128 devices in a mesh: group: 8 (over z, core), local: 16 (over y, x).
Axes of the slice: x: 4, y: 4, z: 4, core: 2. Of those that a mesh axis runs over, the one named last changes fastest.
Arguments:
- hidden_rows: bfloat16 [8192, 3584], P(('group', 'local')), may hold values from -6 to 6
- expert_ids: int32 [8192, 8], P(('group', 'local')), may hold values from 0 to 127, as said below
- route_weights: bfloat16 [8192, 8], P(('group', 'local')), may hold values from 0.099609375 to 1
- w_in: bfloat16 [128, 3584, 2048], P(('group', 'local')), may hold values from -0.09375 to 0.09375
- w_out: bfloat16 [128, 1024, 3584], P(('group', 'local')), may hold values from -0.1875 to 0.1875
Outputs:
- moe_out: bfloat16 [8192, 3584], P(('group', 'local'))
The draws below stay inside these ranges and needn't reach their ends.
Inputs may be any that keep to these rules, and one draw needn't show every extreme that they name: `expert_ids`: each row names 8 different experts: two in each of exactly 4 different node groups. Within the rows of one device (aligned blocks of 64 rows) no node group is named by more than 48 rows and some node group by exactly 48; no expert is named by more than 6 rows and some expert by exactly 6; within one node group, the counts of its experts over the rows of one device differ by at most one.
All inputs are finite; a program needn't handle non-finite values.
Results may differ from the reference program's by a relative error of at most 0.012.
Values may be sent and summed in bfloat16 or wider, within the bound.
No kernel may reach another device: no remote copies, remote signals or barrier semaphores. Data moves between devices by JAX's collectives and lax.ppermute only.
A program may use at most 128 MiB of HBM per device.

```python
import jax
import jax.numpy as jnp
from jax import lax

D = 3584
FFE = 1024
TOP = 8
GSEL = 4
TOK_DEV = 64
EXPERTS = 128
GCAP = 48
CAP = 6
TOKENS = 8192
N_GROUP = 8
N_LOCAL = 16


def local_order(sub_key):
    return jax.random.permutation(sub_key, N_LOCAL)


def route_block(block_key):
    token_key, group_key, local_key = jax.random.split(block_key, 3)
    position = jnp.arange(TOK_DEV, dtype=jnp.int32)
    leading = position < GCAP
    spare = max(N_GROUP - GSEL, 1)
    offset = jnp.where(leading, -(position % GSEL) % N_GROUP, 1 + (position - GCAP) % spare)
    labels = (offset[:, None] + jnp.arange(GSEL, dtype=jnp.int32)[None, :]) % N_GROUP
    relabel = jax.random.permutation(group_key, N_GROUP).astype(jnp.int32)
    groups_all = relabel[labels]
    shuffle = jax.random.permutation(token_key, TOK_DEV).astype(jnp.int32)
    chosen = groups_all[shuffle]
    member = (chosen[:, :, None] == jnp.arange(N_GROUP, dtype=jnp.int32)[None, None, :]).astype(jnp.int32)
    present = jnp.sum(member, axis=1)
    earlier = jnp.cumsum(present, axis=0) - present
    ranking = jnp.sum(member * earlier[:, None, :], axis=2)
    orders = jax.vmap(local_order)(jax.random.split(local_key, N_GROUP)).astype(jnp.int32)
    table = orders[chosen]
    lower = jnp.take_along_axis(table, (2 * ranking % N_LOCAL)[:, :, None], axis=2)[:, :, 0]
    upper = jnp.take_along_axis(table, ((2 * ranking + 1) % N_LOCAL)[:, :, None], axis=2)[:, :, 0]
    experts = jnp.stack([chosen * N_LOCAL + lower, chosen * N_LOCAL + upper], axis=2)
    return experts.reshape(TOK_DEV, GSEL * 2)


def draw_expert_ids(key, part):
    key = jax.random.fold_in(key, 11)
    blocks = TOKENS // TOK_DEV
    block_keys = jax.random.split(key, blocks)
    result = jax.vmap(route_block)(block_keys)
    return result.reshape(TOKENS, TOP).astype(jnp.int32)


def block_levels(rng, extent, cuts, least, high):
    gain, own = 1.0, jax.random.fold_in(rng, 6)
    for dim, shards_of in cuts:
        heights = jnp.exp(jax.random.uniform(jax.random.fold_in(own, dim), (shards_of,), jnp.float32, least / len(cuts), high / len(cuts)))
        gain = gain * jnp.repeat(heights, extent[dim] // shards_of).reshape([-1 if axis == dim else 1 for axis in range(len(extent))])
    return gain


def noise(stream_key, shape, scale, bound, shards=(), kind=jnp.bfloat16):
    drawn = jax.random.normal(stream_key, shape, jnp.float32) * scale
    if len(shards) > 0:
        drawn = block_levels(stream_key, shape, shards, -0.22, 0.18) * drawn
    return jnp.clip(drawn, min=-bound, max=bound).astype(kind)


def setup_inputs(seed: int = 0) -> dict:
    streams_of = jax.random.split(jax.random.key(seed), 6)
    hidden_rows = noise(streams_of[0], (TOKENS, D), 1.0, 6.0, ((0, 128),))
    expert_ids = draw_expert_ids(jax.random.fold_in(streams_of[5], 71), 0)
    route_weights = jnp.clip(0.099609375 + 0.9003906 * jax.random.uniform(streams_of[2], (TOKENS, TOP), jnp.float32) ** block_levels(streams_of[2], (TOKENS, TOP), ((0, 128),), -0.2, 0.2), 0.099609375, 1.0).astype(jnp.bfloat16)
    w_in = noise(streams_of[3], (EXPERTS, D, 2 * FFE), D ** -0.5, 0.09375, ((0, 128),))
    w_out = noise(streams_of[4], (EXPERTS, FFE, D), FFE ** -0.5, 0.1875, ((0, 128),))
    return dict(hidden_rows=hidden_rows, expert_ids=expert_ids, route_weights=route_weights, w_in=w_in, w_out=w_out)


def expert_ffn(rows, first, second):
    both = jnp.dot(rows, first, preferred_element_type=jnp.float32)
    width = first.shape[1] // 2
    inner = (jax.nn.silu(both[:, :width]) * both[:, width:]).astype(jnp.bfloat16)
    return jnp.dot(inner, second, preferred_element_type=jnp.float32).astype(jnp.bfloat16)


def reference(hidden_rows, expert_ids, route_weights, w_in, w_out):
    tokens = hidden_rows.shape[0]
    width = hidden_rows.shape[1]
    limit = min(tokens, N_GROUP * N_LOCAL * CAP)
    weights_f = route_weights.astype(jnp.float32)
    order = jnp.arange(tokens, dtype=jnp.int32)

    def group_step(total, group_index):
        def local_step(local_index, partial_value):
            expert = (group_index * N_LOCAL + local_index).astype(jnp.int32)
            hit = expert_ids == expert
            weight = jnp.sum(jnp.where(hit, weights_f, jnp.float32(0.0)), axis=1)
            routed = jnp.any(hit, axis=1)
            keyed = jnp.where(routed, order, order + tokens).astype(jnp.int32)
            picked = jnp.argsort(keyed)[:limit].astype(jnp.int32)
            result = expert_ffn(hidden_rows[picked], w_in[expert], w_out[expert]).astype(jnp.float32)
            return partial_value.at[picked].add(weight[picked][:, None] * result)

        partial_value = lax.fori_loop(0, N_LOCAL, local_step, jnp.zeros((tokens, width), jnp.float32))
        rounded = lax.optimization_barrier(partial_value.astype(jnp.bfloat16))
        return total + rounded.astype(jnp.float32), None

    total, _ = lax.scan(group_step, jnp.zeros((tokens, width), jnp.float32), jnp.arange(N_GROUP, dtype=jnp.int32))
    return total.astype(jnp.bfloat16)
```

```python
import functools

import jax
import jax.numpy as jnp
from jax import lax
from jax.experimental import pallas as pl
from jax.experimental.pallas import tpu as pltpu
from jax.sharding import PartitionSpec as P

AXES = ("group", "local")
SLOTS = 6
PACKED = 8
HALVES = 2
THIRDS = 3
F32 = jnp.float32
BF16 = jnp.bfloat16


def iota(shape, dim):
    return lax.broadcasted_iota(jnp.int32, shape, dim)


def routing(ids, experts):
    choices, tokens = ids.shape
    twice = jnp.concatenate([ids, ids], axis=1)
    lanes = 2 * tokens
    expert = iota((experts, lanes), 0)
    hit = jnp.zeros((experts, lanes), F32)
    for k in range(choices):
        hit += jnp.where(twice[k : k + 1, :] == expert, 1.0, 0.0)
    row, col = iota((lanes, lanes), 0), iota((lanes, lanes), 1)
    earlier = (row < col) & ((row < tokens) == (col < tokens))
    before = jnp.dot(hit.astype(BF16), jnp.where(earlier, 1.0, 0.0).astype(BF16), preferred_element_type=F32)
    return twice, jnp.where(hit > 0.0, before, -1.0)


def wanted(third, tokens):
    row = iota((PACKED, 2 * tokens), 0)
    head = jnp.where(row < SLOTS, row, -5)
    tail = jnp.where(row < SLOTS, -5, (row - SLOTS) * THIRDS + third)
    return jnp.where(iota((PACKED, 2 * tokens), 1) < tokens, head, tail).astype(F32)


def pack_kernel(ids_ref, head_ref, tail_ref, out_ref, code):
    third = pl.program_id(0)
    experts, lanes = code.shape

    @pl.when(third == 0)
    def _():
        code[...] = routing(ids_ref[...], experts)[1]

    pick = jnp.where(code[...][:, None, :] == wanted(third, lanes // 2)[None], 1.0, 0.0)
    pick = pick.reshape(experts * PACKED, lanes).astype(BF16)
    both = jnp.concatenate([head_ref[...], tail_ref[...]], axis=0)
    out_ref[...] = jnp.dot(pick, both, preferred_element_type=F32).astype(BF16)


def weigh_kernel(ids_ref, weight_ref, out_ref):
    _, experts, lanes = out_ref.shape[0], out_ref.shape[2] // PACKED, out_ref.shape[1]
    twice, code = routing(ids_ref[...], experts)
    weights = weight_ref[...].astype(F32)
    weights = jnp.concatenate([weights, weights], axis=1)
    expert = iota((experts, lanes), 0)
    weight = jnp.zeros((experts, lanes), F32)
    for k in range(twice.shape[0]):
        weight += jnp.where(twice[k : k + 1, :] == expert, weights[k : k + 1, :], 0.0)
    for third in range(THIRDS):
        placed = jnp.where(code[:, None, :] == wanted(third, lanes // 2)[None], weight[:, None, :], 0.0)
        out_ref[third] = placed.reshape(experts * PACKED, lanes).T.astype(BF16)


def combine_kernel(weight_ref, rows_ref, out_ref, tails):
    third = pl.program_id(0)
    tokens = out_ref.shape[0]
    part = rows_ref.shape[1]
    result = jnp.dot(weight_ref[0], rows_ref[...], preferred_element_type=F32)
    out_ref[:, pl.ds(pl.multiple_of(third * part, 128), part)] = result[:tokens].astype(BF16)

    @pl.when(third == 0)
    def _():
        tails[...] = result[tokens:]

    @pl.when(third > 0)
    def _():
        tails[...] += result[tokens:]

    @pl.when(third == THIRDS - 1)
    def _():
        out_ref[:, pl.ds(THIRDS * part, part)] = tails[...].astype(BF16)


BLOCK = 256
SENDERS = BLOCK // PACKED
RUN = SENDERS * HALVES
TILE = 256


def order(transposed):
    to = iota((BLOCK, BLOCK), 1 if transposed else 0)
    source = iota((BLOCK, BLOCK), 0 if transposed else 1)
    run, within = to // RUN, to % RUN
    sender, half = within // HALVES, within % HALVES
    packed = sender * PACKED + jnp.where(run < THIRDS, half * THIRDS + run, SLOTS + half)
    return jnp.where(source == packed, 1.0, 0.0).astype(BF16)


def expert_kernel(rows_ref, first_ref, second_ref, out_ref, packed, first, second, rows, inner, runs, sems):
    count, head = packed.shape
    part = head // THIRDS
    blocks = count // BLOCK
    third_rows = blocks * RUN
    width = rows.shape[1]
    hidden = inner.shape[1]
    tiles = hidden // TILE
    copies = []

    def start(source, target):
        copy = pltpu.make_async_copy(source, target, sems.at[len(copies)])
        copy.start()
        copies.append(copy)
        return copy

    row_copies = [start(rows_ref.at[pl.ds(b * BLOCK, BLOCK)], packed.at[pl.ds(b * BLOCK, BLOCK)]) for b in range(blocks)]
    first_copies = [
        [
            start(first_ref.at[:, pl.ds(at + t * TILE, TILE)], first.at[:, pl.ds(at + t * TILE, TILE)])
            for at in (0, hidden)
        ]
        for t in range(tiles)
    ]
    second_cols = [pl.ds(3 * (width // 4) - TILE // 2, width // 4 + TILE // 2), pl.ds(0, 3 * (width // 4) - TILE // 2)]
    second_copies = [start(second_ref.at[:, c], second.at[:, c]) for c in second_cols]

    forward = order(False)
    for b in range(blocks):
        row_copies[b].wait()
        sorted_rows = jnp.dot(forward, packed[b * BLOCK : (b + 1) * BLOCK, :], preferred_element_type=F32).astype(BF16)
        for k in range(THIRDS):
            at = k * third_rows + b * RUN
            rows[at : at + RUN, :head] = sorted_rows[k * RUN : (k + 1) * RUN, :]
            rows[at : at + RUN, head:] = sorted_rows[THIRDS * RUN :, k * part : (k + 1) * part]

    for t in range(tiles):
        for copy in first_copies[t]:
            copy.wait()
        gate = jnp.dot(rows[...], first[:, t * TILE : (t + 1) * TILE], preferred_element_type=F32)
        up = jnp.dot(rows[...], first[:, hidden + t * TILE : hidden + (t + 1) * TILE], preferred_element_type=F32)
        inner[:, t * TILE : (t + 1) * TILE] = (gate / (1.0 + jnp.exp(-gate)) * up).astype(BF16)

    backward = order(True)

    def down(at):
        result = jnp.dot(inner[...], second[:, at : at + TILE], preferred_element_type=F32).astype(BF16)
        for begin in range(at, at + TILE, TILE // 2):
            cols = result[:, begin - at : begin - at + TILE // 2]
            for b in range(blocks):
                for k in range(THIRDS):
                    piece = cols[k * third_rows + b * RUN : k * third_rows + (b + 1) * RUN]
                    if begin < head:
                        runs[b * BLOCK + k * RUN : b * BLOCK + (k + 1) * RUN, begin : begin + TILE // 2] = piece
                    else:
                        to = k * part + begin - head
                        runs[b * BLOCK + THIRDS * RUN : (b + 1) * BLOCK, to : to + TILE // 2] = piece

    second_copies[0].wait()
    first_tile = (head // TILE) * TILE
    for at in range(first_tile, width, TILE):
        down(at)
    second_copies[1].wait()
    at = 0
    out_copies = []
    for k in range(THIRDS):
        while at < min((k + 1) * part, first_tile):
            down(at)
            at += TILE
        cols = pl.ds(k * part, part)
        for b in range(blocks):
            result = jnp.dot(backward, runs[b * BLOCK : (b + 1) * BLOCK, k * part : (k + 1) * part], preferred_element_type=F32)
            packed[b * BLOCK : (b + 1) * BLOCK, k * part : (k + 1) * part] = result.astype(BF16)
        out_copies.append(start(packed.at[:, cols], out_ref.at[:, cols]))
    for copy in out_copies:
        copy.wait()


def body(hidden_rows, expert_ids, route_weights, w_in, w_out):
    tokens, width = hidden_rows.shape
    choices = expert_ids.shape[1]
    experts = lax.axis_size("group") * lax.axis_size("local")
    part = width // 4
    head = THIRDS * part
    packed_rows = experts * PACKED
    lanes = 2 * tokens
    hidden = w_out.shape[1]
    ids = expert_ids.T
    weights = route_weights.T
    params = functools.partial(pltpu.CompilerParams, vmem_limit_bytes=60 * 1024 * 1024)
    whole = lambda *shape: pl.BlockSpec(shape, lambda k: (0,) * len(shape))

    send = pl.pallas_call(
        pack_kernel,
        grid=(THIRDS,),
        out_shape=jax.ShapeDtypeStruct((packed_rows, head), BF16),
        in_specs=[
            whole(choices, tokens),
            pl.BlockSpec((tokens, part), lambda k: (0, k)),
            pl.BlockSpec((tokens, part), lambda k: (0, THIRDS)),
        ],
        out_specs=pl.BlockSpec((packed_rows, part), lambda k: (0, k)),
        scratch_shapes=[pltpu.VMEM((experts, lanes), F32)],
        compiler_params=params(),
        name="pack",
    )(ids, hidden_rows, hidden_rows)

    received = lax.all_to_all(send, AXES, split_axis=0, concat_axis=0, tiled=True)

    placed = pl.pallas_call(
        weigh_kernel,
        out_shape=jax.ShapeDtypeStruct((THIRDS, lanes, packed_rows), BF16),
        compiler_params=params(),
        cost_estimate=pl.CostEstimate(flops=10**7, bytes_accessed=10**6, transcendentals=0),
        name="weigh",
    )(ids, weights)

    slots = packed_rows * SLOTS // PACKED
    flops = 2 * slots * width * 3 * hidden
    produced = pl.pallas_call(
        expert_kernel,
        out_shape=jax.ShapeDtypeStruct((packed_rows, head), BF16),
        in_specs=[pl.BlockSpec(memory_space=pl.ANY)] * 3,
        out_specs=pl.BlockSpec(memory_space=pl.ANY),
        scratch_shapes=[
            pltpu.VMEM((packed_rows, head), BF16),
            pltpu.VMEM((width, 2 * hidden), BF16),
            pltpu.VMEM((hidden, width), BF16),
            pltpu.VMEM((slots, width), BF16),
            pltpu.VMEM((slots, hidden), BF16),
            pltpu.VMEM((packed_rows, head), BF16),
            pltpu.SemaphoreType.DMA((32,)),
        ],
        compiler_params=params(),
        cost_estimate=pl.CostEstimate(flops=flops, bytes_accessed=33 * 10**6, transcendentals=slots * hidden),
        name="expert",
    )(received, w_in[0], w_out[0])

    returned = lax.all_to_all(produced, AXES, split_axis=0, concat_axis=0, tiled=True)

    return pl.pallas_call(
        combine_kernel,
        grid=(THIRDS,),
        out_shape=jax.ShapeDtypeStruct((tokens, width), BF16),
        in_specs=[
            pl.BlockSpec((1, lanes, packed_rows), lambda k: (k, 0, 0)),
            pl.BlockSpec((packed_rows, part), lambda k: (0, k)),
        ],
        out_specs=whole(tokens, width),
        scratch_shapes=[pltpu.VMEM((tokens, part), F32)],
        compiler_params=params(),
        name="combine",
    )(placed, returned)


def solution(mesh):
    rows = P(AXES, None)
    stacks = P(AXES, None, None)
    return jax.shard_map(
        body, mesh=mesh, in_specs=(rows, rows, rows, stacks, stacks), out_specs=rows, check_vma=False
    )
```

```python
import jax
import jax.numpy as jnp
from jax import lax
from jax.experimental import pallas as pl
from jax.experimental.pallas import tpu as pltpu
from jax.sharding import PartitionSpec as P

AXES = ("group", "local")
SLOTS = 6
PACKED = 8
HALVES = 2
THIRDS = 3
F32 = jnp.float32
BF16 = jnp.bfloat16


def iota(shape, dim):
    return lax.broadcasted_iota(jnp.int32, shape, dim)


def routing(ids, experts):
    choices, tokens = ids.shape
    twice = jnp.concatenate([ids, ids], axis=1)
    lanes = 2 * tokens
    expert = iota((experts, lanes), 0)
    hit = jnp.zeros((experts, lanes), F32)
    for k in range(choices):
        hit += jnp.where(twice[k : k + 1, :] == expert, 1.0, 0.0)
    row, col = iota((lanes, lanes), 0), iota((lanes, lanes), 1)
    earlier = (row < col) & ((row < tokens) == (col < tokens))
    before = jnp.dot(hit.astype(BF16), jnp.where(earlier, 1.0, 0.0).astype(BF16), preferred_element_type=F32)
    return twice, jnp.where(hit > 0.0, before, -1.0)


def wanted(third, tokens):
    row = iota((PACKED, 2 * tokens), 0)
    head = jnp.where(row < SLOTS, row, -5)
    tail = jnp.where(row < SLOTS, -5, (row - SLOTS) * THIRDS + third)
    return jnp.where(iota((PACKED, 2 * tokens), 1) < tokens, head, tail).astype(F32)


def pack_kernel(ids_hbm, weight_hbm, rows_hbm, out_ref, placed_ref, ids, weights, rows, sems):
    tokens, width = rows.shape
    lanes, packed_rows = placed_ref.shape[1:]
    experts = packed_rows // PACKED
    part = width // (THIRDS + 1)
    pairs = ((ids_hbm, ids), (weight_hbm, weights), (rows_hbm, rows))
    copies = [pltpu.make_async_copy(source, target, sems.at[i]) for i, (source, target) in enumerate(pairs)]
    for copy in copies:
        copy.start()
    copies[0].wait()
    twice, code = routing(ids[...], experts)
    hits = [code[:, None, :] == wanted(third, tokens)[None] for third in range(THIRDS)]
    copies[2].wait()
    for third in range(THIRDS):
        pick = jnp.where(hits[third], 1.0, 0.0).reshape(packed_rows, lanes).astype(BF16)
        both = jnp.concatenate([rows[:, third * part : (third + 1) * part], rows[:, THIRDS * part :]], axis=0)
        out_ref[:, third * part : (third + 1) * part] = jnp.dot(pick, both, preferred_element_type=F32).astype(BF16)
    copies[1].wait()
    factors = weights[...].astype(F32)
    factors = jnp.concatenate([factors, factors], axis=1)
    expert = iota((experts, lanes), 0)
    weight = jnp.zeros((experts, lanes), F32)
    for k in range(twice.shape[0]):
        weight += jnp.where(twice[k : k + 1, :] == expert, factors[k : k + 1, :], 0.0)
    for third in range(THIRDS):
        placed = jnp.where(hits[third], weight[:, None, :], 0.0)
        placed_ref[third] = placed.reshape(packed_rows, lanes).T.astype(BF16)


def combine_kernel(weight_ref, rows_ref, out_ref):
    tokens, width = out_ref.shape
    part = width // (THIRDS + 1)
    tails = jnp.zeros((tokens, part), F32)
    for third in range(THIRDS):
        cols = slice(third * part, (third + 1) * part)
        result = jnp.dot(weight_ref[third], rows_ref[:, cols], preferred_element_type=F32)
        out_ref[:, cols] = result[:tokens].astype(BF16)
        tails += result[tokens:]
    out_ref[:, THIRDS * part :] = tails.astype(BF16)


BLOCK = 256
SENDERS = BLOCK // PACKED
RUN = SENDERS * HALVES
TILE = 256


def order(transposed):
    to = iota((BLOCK, BLOCK), 1 if transposed else 0)
    source = iota((BLOCK, BLOCK), 0 if transposed else 1)
    run, within = to // RUN, to % RUN
    sender, half = within // HALVES, within % HALVES
    packed = sender * PACKED + jnp.where(run < THIRDS, half * THIRDS + run, SLOTS + half)
    return jnp.where(source == packed, 1.0, 0.0).astype(BF16)


def expert_kernel(packed, first_hbm, second_hbm, out_ref, first, second, rows, inner, runs, sems):
    count, head = packed.shape
    part = head // THIRDS
    blocks = count // BLOCK
    third_rows = blocks * RUN
    width = rows.shape[1]
    hidden = inner.shape[1]
    tiles = hidden // TILE
    split = (head // TILE) * TILE

    def fetch(source, target, cols, sem):
        copy = pltpu.make_async_copy(source.at[:, cols], target.at[:, cols], sems.at[sem])
        copy.start()
        return copy

    first_copies = [
        [fetch(first_hbm, first, pl.ds(at + t * TILE, TILE), 2 * t + i) for i, at in enumerate((0, hidden))]
        for t in range(tiles)
    ]
    second_copies = [
        fetch(second_hbm, second, pl.ds(split, width - split), 2 * tiles),
        fetch(second_hbm, second, pl.ds(0, split), 2 * tiles + 1),
    ]

    forward = order(False)
    for b in range(blocks):
        sorted_rows = jnp.dot(forward, packed[b * BLOCK : (b + 1) * BLOCK, :], preferred_element_type=F32).astype(BF16)
        for k in range(THIRDS):
            at = k * third_rows + b * RUN
            rows[at : at + RUN, :head] = sorted_rows[k * RUN : (k + 1) * RUN, :]
            rows[at : at + RUN, head:] = sorted_rows[THIRDS * RUN :, k * part : (k + 1) * part]

    for t in range(tiles):
        for copy in first_copies[t]:
            copy.wait()
        gate = jnp.dot(rows[...], first[:, t * TILE : (t + 1) * TILE], preferred_element_type=F32)
        up = jnp.dot(rows[...], first[:, hidden + t * TILE : hidden + (t + 1) * TILE], preferred_element_type=F32)
        inner[:, t * TILE : (t + 1) * TILE] = (gate / (1.0 + jnp.exp(-gate)) * up).astype(BF16)

    backward = order(True)

    def down(at):
        result = jnp.dot(inner[...], second[:, at : at + TILE], preferred_element_type=F32).astype(BF16)
        for begin in range(at, at + TILE, TILE // 2):
            cols = result[:, begin - at : begin - at + TILE // 2]
            for b in range(blocks):
                for k in range(THIRDS):
                    piece = cols[k * third_rows + b * RUN : k * third_rows + (b + 1) * RUN]
                    if begin < head:
                        runs[b * BLOCK + k * RUN : b * BLOCK + (k + 1) * RUN, begin : begin + TILE // 2] = piece
                    else:
                        to = k * part + begin - head
                        runs[b * BLOCK + THIRDS * RUN : (b + 1) * BLOCK, to : to + TILE // 2] = piece

    second_copies[0].wait()
    for at in range(split, width, TILE):
        down(at)
    second_copies[1].wait()
    at = 0
    for k in range(THIRDS):
        while at < min((k + 1) * part, split):
            down(at)
            at += TILE
        cols = slice(k * part, (k + 1) * part)
        for b in range(blocks):
            block = slice(b * BLOCK, (b + 1) * BLOCK)
            out_ref[block, cols] = jnp.dot(backward, runs[block, cols], preferred_element_type=F32).astype(BF16)


def body(hidden_rows, expert_ids, route_weights, w_in, w_out):
    tokens, width = hidden_rows.shape
    choices = expert_ids.shape[1]
    experts = lax.axis_size("group") * lax.axis_size("local")
    head = THIRDS * (width // 4)
    packed_rows = experts * PACKED
    slots = experts * SLOTS
    lanes = 2 * tokens
    hidden = w_out.shape[1]
    near = pl.BlockSpec(memory_space=pltpu.VMEM)
    far = pl.BlockSpec(memory_space=pltpu.HBM)
    limit = lambda mib: pltpu.CompilerParams(vmem_limit_bytes=mib * 2**20)
    exchange = lambda rows: lax.all_to_all(rows, AXES, split_axis=0, concat_axis=0, tiled=True)
    packed = jax.ShapeDtypeStruct((packed_rows, head), BF16)

    send, placed = pl.pallas_call(
        pack_kernel,
        out_shape=(packed, jax.ShapeDtypeStruct((THIRDS, lanes, packed_rows), BF16)),
        in_specs=[far] * 3,
        out_specs=(near, near),
        scratch_shapes=[
            pltpu.VMEM((choices, tokens), jnp.int32),
            pltpu.VMEM((choices, tokens), BF16),
            pltpu.VMEM((tokens, width), BF16),
            pltpu.SemaphoreType.DMA((3,)),
        ],
        compiler_params=limit(16),
        name="pack",
    )(expert_ids.T, route_weights.T, hidden_rows)

    produced = pl.pallas_call(
        expert_kernel,
        out_shape=packed,
        in_specs=[near, far, far],
        out_specs=near,
        scratch_shapes=[
            pltpu.VMEM((width, 2 * hidden), BF16),
            pltpu.VMEM((hidden, width), BF16),
            pltpu.VMEM((slots, width), BF16),
            pltpu.VMEM((slots, hidden), BF16),
            pltpu.VMEM((packed_rows, head), BF16),
            pltpu.SemaphoreType.DMA((2 * hidden // TILE + 2,)),
        ],
        compiler_params=limit(42),
        name="expert",
    )(exchange(send), w_in[0], w_out[0])

    return pl.pallas_call(
        combine_kernel,
        out_shape=jax.ShapeDtypeStruct((tokens, width), BF16),
        in_specs=[near, near],
        out_specs=near,
        compiler_params=limit(16),
        name="combine",
    )(placed, exchange(produced))


def solution(mesh):
    rows = P(AXES, None)
    stacks = P(AXES, None, None)
    return jax.shard_map(
        body, mesh=mesh, in_specs=(rows, rows, rows, stacks, stacks), out_specs=rows, check_vma=False
    )
```

```python
import jax
import jax.numpy as jnp
from jax import lax
from jax.experimental import pallas as pl
from jax.experimental.pallas import tpu as pltpu
from jax.sharding import PartitionSpec as P

AXES = ("group", "local")
SLOTS = 6
PACKED = 8
HALVES = 2
THIRDS = 3
F32 = jnp.float32
BF16 = jnp.bfloat16


def iota(shape, dim):
    return lax.broadcasted_iota(jnp.int32, shape, dim)


def routing(ids, experts):
    choices, tokens = ids.shape
    twice = jnp.concatenate([ids, ids], axis=1)
    lanes = 2 * tokens
    expert = iota((experts, lanes), 0)
    hit = jnp.zeros((experts, lanes), F32)
    for k in range(choices):
        hit += jnp.where(twice[k : k + 1, :] == expert, 1.0, 0.0)
    row, col = iota((lanes, lanes), 0), iota((lanes, lanes), 1)
    earlier = (row < col) & ((row < tokens) == (col < tokens))
    before = jnp.dot(hit.astype(BF16), jnp.where(earlier, 1.0, 0.0).astype(BF16), preferred_element_type=F32)
    return twice, jnp.where(hit > 0.0, before, -1.0)


def wanted(third, tokens):
    row = iota((PACKED, 2 * tokens), 0)
    head = jnp.where(row < SLOTS, row, -5)
    tail = jnp.where(row < SLOTS, -5, (row - SLOTS) * THIRDS + third)
    return jnp.where(iota((PACKED, 2 * tokens), 1) < tokens, head, tail).astype(F32)


def pack_kernel(ids_ref, rows_ref, out_ref):
    tokens, width = rows_ref.shape
    packed_rows = out_ref.shape[0]
    part = width // (THIRDS + 1)
    code = routing(ids_ref[...], packed_rows // PACKED)[1]
    for third in range(THIRDS):
        pick = jnp.where(code[:, None, :] == wanted(third, tokens)[None], 1.0, 0.0)
        pick = pick.reshape(packed_rows, 2 * tokens).astype(BF16)
        both = jnp.concatenate([rows_ref[:, third * part : (third + 1) * part], rows_ref[:, THIRDS * part :]], axis=0)
        out_ref[:, third * part : (third + 1) * part] = jnp.dot(pick, both, preferred_element_type=F32).astype(BF16)


def weigh(ids, weights, placed_ref):
    lanes, packed_rows = placed_ref.shape[1:]
    experts = packed_rows // PACKED
    twice, code = routing(ids, experts)
    factors = weights.astype(F32)
    factors = jnp.concatenate([factors, factors], axis=1)
    expert = iota((experts, lanes), 0)
    weight = jnp.zeros((experts, lanes), F32)
    for k in range(twice.shape[0]):
        weight += jnp.where(twice[k : k + 1, :] == expert, factors[k : k + 1, :], 0.0)
    for third in range(THIRDS):
        hit = code[:, None, :] == wanted(third, lanes // 2)[None]
        placed = jnp.where(hit, weight[:, None, :], 0.0)
        placed_ref[third] = placed.reshape(packed_rows, lanes).T.astype(BF16)


def combine_kernel(weight_ref, rows_ref, out_ref):
    tokens, width = out_ref.shape
    part = width // (THIRDS + 1)
    tails = jnp.zeros((tokens, part), F32)
    for third in range(THIRDS):
        cols = slice(third * part, (third + 1) * part)
        result = jnp.dot(weight_ref[third], rows_ref[:, cols], preferred_element_type=F32)
        out_ref[:, cols] = result[:tokens].astype(BF16)
        tails += result[tokens:]
    out_ref[:, THIRDS * part :] = tails.astype(BF16)


BLOCK = 256
SENDERS = BLOCK // PACKED
RUN = SENDERS * HALVES
TILE = 256


def order(transposed):
    to = iota((BLOCK, BLOCK), 1 if transposed else 0)
    source = iota((BLOCK, BLOCK), 0 if transposed else 1)
    run, within = to // RUN, to % RUN
    sender, half = within // HALVES, within % HALVES
    packed = sender * PACKED + jnp.where(run < THIRDS, half * THIRDS + run, SLOTS + half)
    return jnp.where(source == packed, 1.0, 0.0).astype(BF16)


def expert_kernel(packed, first, second, ids_ref, weight_ref, out_ref, placed_ref, rows, inner, runs):
    count, head = packed.shape
    part = head // THIRDS
    blocks = count // BLOCK
    third_rows = blocks * RUN
    width = rows.shape[1]
    hidden = inner.shape[1]
    tiles = hidden // TILE
    split = (head // TILE) * TILE

    forward = order(False)
    for b in range(blocks):
        sorted_rows = jnp.dot(forward, packed[b * BLOCK : (b + 1) * BLOCK, :], preferred_element_type=F32).astype(BF16)
        for k in range(THIRDS):
            at = k * third_rows + b * RUN
            rows[at : at + RUN, :head] = sorted_rows[k * RUN : (k + 1) * RUN, :]
            rows[at : at + RUN, head:] = sorted_rows[THIRDS * RUN :, k * part : (k + 1) * part]

    for t in range(tiles):
        gate = jnp.dot(rows[...], first[:, t * TILE : (t + 1) * TILE], preferred_element_type=F32)
        up = jnp.dot(rows[...], first[:, hidden + t * TILE : hidden + (t + 1) * TILE], preferred_element_type=F32)
        inner[:, t * TILE : (t + 1) * TILE] = (gate / (1.0 + jnp.exp(-gate)) * up).astype(BF16)

    weigh(ids_ref[...], weight_ref[...], placed_ref)
    backward = order(True)

    def down(at):
        result = jnp.dot(inner[...], second[:, at : at + TILE], preferred_element_type=F32).astype(BF16)
        for begin in range(at, at + TILE, TILE // 2):
            cols = result[:, begin - at : begin - at + TILE // 2]
            for b in range(blocks):
                for k in range(THIRDS):
                    piece = cols[k * third_rows + b * RUN : k * third_rows + (b + 1) * RUN]
                    if begin < head:
                        runs[b * BLOCK + k * RUN : b * BLOCK + (k + 1) * RUN, begin : begin + TILE // 2] = piece
                    else:
                        to = k * part + begin - head
                        runs[b * BLOCK + THIRDS * RUN : (b + 1) * BLOCK, to : to + TILE // 2] = piece

    for at in range(split, width, TILE):
        down(at)
    at = 0
    for k in range(THIRDS):
        while at < min((k + 1) * part, split):
            down(at)
            at += TILE
        cols = slice(k * part, (k + 1) * part)
        for b in range(blocks):
            block = slice(b * BLOCK, (b + 1) * BLOCK)
            out_ref[block, cols] = jnp.dot(backward, runs[block, cols], preferred_element_type=F32).astype(BF16)


def body(hidden_rows, expert_ids, route_weights, w_in, w_out):
    tokens, width = hidden_rows.shape
    experts = lax.axis_size("group") * lax.axis_size("local")
    head = THIRDS * (width // 4)
    packed_rows = experts * PACKED
    slots = experts * SLOTS
    lanes = 2 * tokens
    hidden = w_out.shape[1]
    near = pl.BlockSpec(memory_space=pltpu.VMEM)
    far = pl.BlockSpec(memory_space=pltpu.HBM)
    limit = lambda mib: pltpu.CompilerParams(vmem_limit_bytes=mib * 2**20)
    exchange = lambda rows: lax.all_to_all(rows, AXES, split_axis=0, concat_axis=0, tiled=True)
    packed = jax.ShapeDtypeStruct((packed_rows, head), BF16)

    ids, weights = expert_ids.T, route_weights.T
    send = pl.pallas_call(
        pack_kernel,
        out_shape=packed,
        in_specs=[near] * 2,
        out_specs=near,
        compiler_params=limit(16),
        cost_estimate=pl.CostEstimate(flops=10**11, bytes_accessed=10**7, transcendentals=0),
        name="pack",
    )(ids, hidden_rows)

    produced, placed = pl.pallas_call(
        expert_kernel,
        out_shape=(packed, jax.ShapeDtypeStruct((THIRDS, lanes, packed_rows), BF16)),
        in_specs=[near] * 5,
        out_specs=(near, near),
        scratch_shapes=[
            pltpu.VMEM((slots, width), BF16),
            pltpu.VMEM((slots, hidden), BF16),
            pltpu.VMEM((packed_rows, head), BF16),
        ],
        compiler_params=limit(18),
        name="expert",
    )(exchange(send), w_in[0], w_out[0], ids, weights)

    return pl.pallas_call(
        combine_kernel,
        out_shape=jax.ShapeDtypeStruct((tokens, width), BF16),
        in_specs=[near, near],
        out_specs=near,
        compiler_params=limit(16),
        name="combine",
    )(placed, exchange(produced))


def solution(mesh):
    rows = P(AXES, None)
    stacks = P(AXES, None, None)
    return jax.shard_map(
        body, mesh=mesh, in_specs=(rows, rows, rows, stacks, stacks), out_specs=rows, check_vma=False
    )
```

```python
import jax
import jax.numpy as jnp
from jax import lax
from jax.experimental import pallas as pl
from jax.experimental.pallas import tpu as pltpu
from jax.sharding import PartitionSpec as P

AXES = ("group", "local")
SLOTS = 6
PACKED = 8
HALVES = 2
THIRDS = 3
F32 = jnp.float32
BF16 = jnp.bfloat16


def iota(shape, dim):
    return lax.broadcasted_iota(jnp.int32, shape, dim)


def routing(ids, experts):
    choices, tokens = ids.shape
    twice = jnp.concatenate([ids, ids], axis=1)
    lanes = 2 * tokens
    expert = iota((experts, lanes), 0)
    hit = jnp.zeros((experts, lanes), F32)
    for k in range(choices):
        hit += jnp.where(twice[k : k + 1, :] == expert, 1.0, 0.0)
    row, col = iota((lanes, lanes), 0), iota((lanes, lanes), 1)
    earlier = (row < col) & ((row < tokens) == (col < tokens))
    before = jnp.dot(hit.astype(BF16), jnp.where(earlier, 1.0, 0.0).astype(BF16), preferred_element_type=F32)
    return twice, jnp.where(hit > 0.0, before, -1.0)


def wanted(third, tokens):
    row = iota((PACKED, 2 * tokens), 0)
    head = jnp.where(row < SLOTS, row, -5)
    tail = jnp.where(row < SLOTS, -5, (row - SLOTS) * THIRDS + third)
    return jnp.where(iota((PACKED, 2 * tokens), 1) < tokens, head, tail).astype(F32)


def pack_kernel(ids_ref, rows_ref, out_ref):
    tokens, width = rows_ref.shape
    packed_rows = out_ref.shape[0]
    part = width // (THIRDS + 1)
    code = routing(ids_ref[...], packed_rows // PACKED)[1]
    for third in range(THIRDS):
        pick = jnp.where(code[:, None, :] == wanted(third, tokens)[None], 1.0, 0.0)
        pick = pick.reshape(packed_rows, 2 * tokens).astype(BF16)
        both = jnp.concatenate([rows_ref[:, third * part : (third + 1) * part], rows_ref[:, THIRDS * part :]], axis=0)
        out_ref[:, third * part : (third + 1) * part] = jnp.dot(pick, both, preferred_element_type=F32).astype(BF16)


def weigh(ids, weights, placed_ref):
    lanes, packed_rows = placed_ref.shape[1:]
    experts = packed_rows // PACKED
    twice, code = routing(ids, experts)
    factors = weights.astype(F32)
    factors = jnp.concatenate([factors, factors], axis=1)
    expert = iota((experts, lanes), 0)
    weight = jnp.zeros((experts, lanes), F32)
    for k in range(twice.shape[0]):
        weight += jnp.where(twice[k : k + 1, :] == expert, factors[k : k + 1, :], 0.0)
    for third in range(THIRDS):
        hit = code[:, None, :] == wanted(third, lanes // 2)[None]
        placed = jnp.where(hit, weight[:, None, :], 0.0)
        placed_ref[third] = placed.reshape(packed_rows, lanes).T.astype(BF16)


def combine_kernel(weight_ref, rows_ref, out_ref):
    tokens, width = out_ref.shape
    part = width // (THIRDS + 1)
    tails = jnp.zeros((tokens, part), F32)
    for third in range(THIRDS):
        cols = slice(third * part, (third + 1) * part)
        result = jnp.dot(weight_ref[third], rows_ref[:, cols], preferred_element_type=F32)
        out_ref[:, cols] = result[:tokens].astype(BF16)
        tails += result[tokens:]
    out_ref[:, THIRDS * part :] = tails.astype(BF16)


BLOCK = 256
SENDERS = BLOCK // PACKED
RUN = SENDERS * HALVES
TILE = 256


def order():
    to, source = iota((BLOCK, BLOCK), 0), iota((BLOCK, BLOCK), 1)
    run, within = to // RUN, to % RUN
    half, sender = within // SENDERS, within % SENDERS
    packed = sender * PACKED + jnp.where(run < THIRDS, half * THIRDS + run, SLOTS + half)
    return jnp.where(source == packed, 1.0, 0.0).astype(BF16)


def expert_kernel(packed, first, second, ids_ref, weight_ref, out_ref, placed_ref, rows, inner, runs, tails):
    count, head = packed.shape
    part = head // THIRDS
    blocks = count // BLOCK
    width = rows.shape[1]
    hidden = inner.shape[1]
    tiles = hidden // TILE

    lanes = runs.shape[-1]
    strips = part // lanes
    third_rows = THIRDS * RUN

    def sort_by_product(b):
        result = jnp.dot(forward, packed[b * BLOCK : (b + 1) * BLOCK, :], preferred_element_type=F32).astype(BF16)
        for k in range(THIRDS):
            at = b * third_rows + k * RUN
            rows[at : at + RUN, :head] = result[k * RUN : (k + 1) * RUN, :]
            rows[at : at + RUN, head:] = result[THIRDS * RUN :, k * part : (k + 1) * part]

    def sort_by_loads(b):
        per = runs.shape[2] // BLOCK
        for strip in range(head // lanes):
            at = strip % per * BLOCK
            cols = slice(strip * lanes, (strip + 1) * lanes)
            runs[b % 2, strip // per, at : at + BLOCK, :] = packed[b * BLOCK : (b + 1) * BLOCK, cols].astype(F32)

            def take(row, at=at, strip=strip):
                return runs[b % 2, strip // per, pl.ds(at + row, SENDERS, stride=PACKED), :].astype(BF16)

            for half in range(HALVES):
                for k in range(THIRDS):
                    to = b * third_rows + k * RUN + half * SENDERS
                    rows[to : to + SENDERS, cols] = take(half * THIRDS + k)
                k = strip // strips
                to = b * third_rows + k * RUN + half * SENDERS
                begin = head + strip % strips * lanes
                rows[to : to + SENDERS, begin : begin + lanes] = take(SLOTS + half)

    def widen(m, t):
        group = slice(m * count_rows, (m + 1) * count_rows)
        gate = jnp.dot(rows[group, :], first[:, t * TILE : (t + 1) * TILE], preferred_element_type=F32)
        up = jnp.dot(rows[group, :], first[:, hidden + t * TILE : hidden + (t + 1) * TILE], preferred_element_type=F32)
        inner[group, t * TILE : (t + 1) * TILE] = (gate / (1.0 + jnp.exp(-gate)) * up).astype(BF16)

    forward = order()
    count_rows = rows.shape[0] // 2
    for b in range(blocks // 2):
        sort_by_product(b)
    for t in range(tiles):
        widen(0, t)
        if t < blocks - blocks // 2:
            sort_by_loads(blocks // 2 + t)
    for t in range(tiles):
        widen(1, t)

    weigh(ids_ref[...], weight_ref[...], placed_ref)
    def spread(third, strip, row, value, k):
        for b in range(blocks):
            for half in range(HALVES):
                at = b * third_rows + k * RUN + half * SENDERS
                to = pl.ds(b * BLOCK + row(half), SENDERS, stride=PACKED)
                runs[third % 2, strip, to, :] = value[at : at + SENDERS]

    def down(at, end):
        result = jnp.dot(inner[...], second[:, at:end], preferred_element_type=F32)
        for begin in range(at, end, lanes):
            piece = result[:, begin - at : begin - at + lanes]
            if begin >= head:
                tails[:, begin - head : begin - head + lanes] = piece
                continue
            for k in range(THIRDS):
                spread(begin // part, begin % part // lanes, lambda half, k=k: half * THIRDS + k, piece, k)

    for at in range(head, width, TILE):
        down(at, min(at + TILE, width))
    at = 0
    for k in range(THIRDS):
        while at < (k + 1) * part:
            down(at, min(at + TILE, head))
            at += TILE
        for strip in range(strips):
            cols = slice(strip * lanes, (strip + 1) * lanes)
            spread(k, strip, lambda half: SLOTS + half, tails[:, cols], k)
            begin = k * part + strip * lanes
            out_ref[:, begin : begin + lanes] = runs[k % 2, strip].astype(BF16)


def body(hidden_rows, expert_ids, route_weights, w_in, w_out):
    tokens, width = hidden_rows.shape
    experts = lax.axis_size("group") * lax.axis_size("local")
    head = THIRDS * (width // 4)
    packed_rows = experts * PACKED
    slots = experts * SLOTS
    lanes = 2 * tokens
    hidden = w_out.shape[1]
    near = pl.BlockSpec(memory_space=pltpu.VMEM)
    far = pl.BlockSpec(memory_space=pltpu.HBM)
    limit = lambda mib: pltpu.CompilerParams(vmem_limit_bytes=mib * 2**20)
    exchange = lambda rows: lax.all_to_all(rows, AXES, split_axis=0, concat_axis=0, tiled=True)
    packed = jax.ShapeDtypeStruct((packed_rows, head), BF16)

    ids, weights = expert_ids.T, route_weights.T
    send = pl.pallas_call(
        pack_kernel,
        out_shape=packed,
        in_specs=[near] * 2,
        out_specs=near,
        compiler_params=limit(16),
        cost_estimate=pl.CostEstimate(flops=10**11, bytes_accessed=10**7, transcendentals=0),
        name="pack",
    )(ids, hidden_rows)

    produced, placed = pl.pallas_call(
        expert_kernel,
        out_shape=(packed, jax.ShapeDtypeStruct((THIRDS, lanes, packed_rows), BF16)),
        in_specs=[near] * 5,
        out_specs=(near, near),
        scratch_shapes=[
            pltpu.VMEM((slots, width), BF16),
            pltpu.VMEM((slots, hidden), BF16),
            pltpu.VMEM((2, width // 4 // 128, packed_rows, 128), F32),
            pltpu.VMEM((slots, width // 4), F32),
        ],
        compiler_params=limit(20),
        name="expert",
    )(exchange(send), w_in[0], w_out[0], ids, weights)

    return pl.pallas_call(
        combine_kernel,
        out_shape=jax.ShapeDtypeStruct((tokens, width), BF16),
        in_specs=[near, near],
        out_specs=near,
        compiler_params=limit(16),
        name="combine",
    )(placed, exchange(produced))


def solution(mesh):
    rows = P(AXES, None)
    stacks = P(AXES, None, None)
    return jax.shard_map(
        body, mesh=mesh, in_specs=(rows, rows, rows, stacks, stacks), out_specs=rows, check_vma=False
    )
```
